256 devices in a mesh: grp: 4 (over x), sub: 64 (over y, z, core).
Axes of the slice: x: 4, y: 4, z: 8, core: 2. Of those that a mesh axis runs over, the one named last changes fastest.
Arguments:
- blocks: bfloat16 [4, 64, 2048, 2048], P('grp', 'sub'), may hold values from -0.125 to 0.125
- own_vectors: bfloat16 [4, 64, 48, 2048], P('grp', 'sub'), may hold values from -0.890625 to 0.890625
- over_vectors: bfloat16 [4, 64, 8, 4, 48, 128], P('grp', 'sub'), may hold values from -0.890625 to 0.890625
- neighbours: int32 [4, 64, 8], P('grp', 'sub'), may hold values from -1 to 63, as said below
- counts: int32 [4, 64, 8], P('grp', 'sub'), may hold values from 0 to 4, as said below
- margin_rows: int32 [4, 64, 8, 4, 128], P('grp', 'sub'), may hold values from 0 to 2047, as said below
Outputs:
- coarse: float32 [4, 64, 48, 816], P(None, 'sub')
The draws below stay inside these ranges and needn't reach their ends.
Inputs may be any that keep to these rules, and one draw needn't show every extreme that they name: `neighbours`: each entry is -1 or the number of a subdomain of the same group at distance 1 to 4 from the listing subdomain; no number twice in a list; the subdomains at distance 1 are always listed when they exist. `counts`: 0 exactly for empty slots, 1 or more for listed neighbours; a subdomain always sends 4 blocks to the subdomain after it. `margin_rows`: within one owner and offset, all 512 rows are distinct.
All inputs are finite; a program needn't handle non-finite values.
Results may differ from the reference program's by a relative error of at most 0.0029.
Values may be sent and summed in bfloat16 or wider, within the bound.
No kernel may reach another device: no remote copies, remote signals or barrier semaphores. Data moves between devices by JAX's collectives and lax.ppermute only.
A program may use at most 128 MiB of HBM per device.

```python
import jax
import jax.numpy as jnp
from jax import lax

K = 48
R = 2048
TILE = 128
MAXT = 4
H = 4
GROUPS = 4
SUBS = 64
N_GRP = 4
N_SUB = 64


def neighbour_table(key):
    offsets = jnp.concatenate([jnp.arange(-H, 0), jnp.arange(1, H + 1)]).astype(jnp.int32)
    device_ids = jnp.arange(SUBS, dtype=jnp.int32)
    target = device_ids[:, None] + offsets[None, :]
    inside = (target >= 0) & (target < SUBS)
    coin = jax.random.randint(jax.random.fold_in(key, 11), (GROUPS, SUBS, 2 * H), 0, 2) == 1
    present = inside[None] & ((jnp.abs(offsets)[None, None, :] == 1) | coin)
    tiles = jax.random.randint(jax.random.fold_in(key, 12), (GROUPS, SUBS, 2 * H), 1, MAXT + 1)
    tiles = jnp.where(offsets[None, None, :] == 1, MAXT, tiles)
    listed = jnp.where(present, jnp.broadcast_to(target[None], present.shape), -1)
    amount = jnp.where(present, tiles, 0)
    scores = jax.random.randint(jax.random.fold_in(key, 13), (GROUPS, SUBS, 2 * H), 0, 1024) * (2 * H) + jnp.arange(2 * H)
    order = jnp.argsort(scores, axis=-1, stable=True)
    listed = jnp.take_along_axis(listed, order, axis=-1)
    amount = jnp.take_along_axis(amount, order, axis=-1)
    return (listed.astype(jnp.int32), amount.astype(jnp.int32))


def draw_neighbours(key, part):
    listed, amount = neighbour_table(key)
    return listed


def draw_counts(key, part):
    listed, amount = neighbour_table(key)
    return amount


def draw_margin_rows(key, part):
    key = jax.random.fold_in(key, 7)
    keys = jax.random.split(key, GROUPS * SUBS * 2 * H)
    chosen = jax.vmap(lambda single: jax.random.permutation(single, R)[:MAXT * TILE])(keys)
    return chosen.reshape(GROUPS, SUBS, 2 * H, MAXT, TILE).astype(jnp.int32)


def shard_levels(rng, shape, pieces, smallest, high):
    level, own = 1.0, jax.random.fold_in(rng, 6)
    for dim, parts in pieces:
        draws = jnp.exp(jax.random.uniform(jax.random.fold_in(own, dim), (parts,), jnp.float32, smallest / len(pieces), high / len(pieces)))
        level = level * jnp.repeat(draws, shape[dim] // parts).reshape([-1 if axis == dim else 1 for axis in range(len(shape))])
    return level


def noise(rng, extent, width, reach, pieces=(), kind=jnp.bfloat16):
    result = width * jax.random.normal(rng, extent, jnp.float32)
    if pieces:
        result = result * shard_levels(rng, extent, pieces, -0.22, 0.18)
    return jnp.clip(result, -reach, reach).astype(kind)


def setup_inputs(seed: int = 0) -> dict:
    streams_of = jax.random.split(jax.random.key(seed), 7)
    blocks = noise(streams_of[0], (GROUPS, SUBS, R, R), R ** -0.5, 0.125, ((0, 4), (1, 64)))
    own_vectors = noise(streams_of[1], (GROUPS, SUBS, K, R), (R ** -0.25), 0.890625, ((0, 4), (1, 64)))
    over_vectors = noise(streams_of[2], (GROUPS, SUBS, 2 * H, MAXT, K, TILE), (R ** -0.25), 0.890625, ((0, 4), (1, 64)))
    neighbours = draw_neighbours(jax.random.fold_in(streams_of[6], 71), 0)
    counts = draw_counts(jax.random.fold_in(streams_of[6], 71), 0)
    margin_rows = draw_margin_rows(jax.random.fold_in(streams_of[6], 71), 0)
    return dict(blocks=blocks, own_vectors=own_vectors, over_vectors=over_vectors, neighbours=neighbours, counts=counts, margin_rows=margin_rows)


def reference(blocks, own_vectors, over_vectors, neighbours, counts, margin_rows):
    span = 2 * H + 1
    tile_index = jnp.arange(MAXT, dtype=jnp.int32)
    live = (tile_index[None, None, None, :] < counts[..., None]).astype(jnp.bfloat16)
    outgoing = over_vectors * live[..., None, None]
    padded_out = jnp.pad(outgoing, ((0, 0), (H, H), (0, 0), (0, 0), (0, 0), (0, 0)))
    padded_list = jnp.pad(neighbours, ((0, 0), (H, H), (0, 0)), constant_values=-1)

    def owner(flat_index):
        group = flat_index // N_SUB
        local = flat_index % N_SUB
        matrix = blocks[group, local]
        stacks = []
        for offset in range(-H, H + 1):
            if offset == 0:
                stacks.append(own_vectors[group, local])
                continue
            slot = offset + H if offset < 0 else offset + H - 1
            sender = (local + offset + H).astype(jnp.int32)
            slots = lax.dynamic_index_in_dim(padded_out[group], sender, 0, keepdims=False)
            listed = lax.dynamic_index_in_dim(padded_list[group], sender, 0, keepdims=False)
            picked = (listed == local).astype(jnp.float32)
            values = jnp.einsum("n,ntkc->tkc", picked, slots.astype(jnp.float32)).astype(jnp.bfloat16)
            rows = margin_rows[group, local, slot]
            flat = jnp.transpose(values, (1, 0, 2)).reshape(K, MAXT * TILE)
            stacks.append(jnp.zeros((K, R), jnp.bfloat16).at[:, rows.reshape(-1)].set(flat))
        present = jnp.concatenate(stacks, axis=0)
        product = jnp.dot(present, matrix, preferred_element_type=jnp.float32).astype(jnp.bfloat16)
        return lax.dot_general(product, present, (((1,), (1,)), ((), ())), preferred_element_type=jnp.float32)

    grams = lax.map(owner, jnp.arange(N_GRP * N_SUB, dtype=jnp.int32))
    grams = grams.reshape(N_GRP, N_SUB, span, K, span * K)
    coarse = jnp.zeros((N_GRP, N_SUB, K, (4 * H + 1) * K), jnp.float32)
    for position in range(span):
        offset = position - H
        row_block = jnp.pad(grams[:, :, position], ((0, 0), (H, H), (0, 0), (0, 0)))
        shifted = row_block[:, H - offset:H - offset + N_SUB]
        start = (H - offset) * K
        coarse = coarse.at[:, :, :, start:start + span * K].add(shifted)
    return coarse
```

```python
import jax
import jax.numpy as jnp
from jax import lax
from jax.experimental import pallas as pl
from jax.experimental.pallas import tpu as pltpu
from jax.sharding import PartitionSpec as P

H = 4
SPAN = 2 * H + 1
WIDE = SPAN + 1
FULL = 4 * H + 1
STACK = (0, 1, 2, 3, 4, -1, -2, -3, -4)
VMEM = pl.BlockSpec(memory_space=pltpu.VMEM)
SMEM = pl.BlockSpec(memory_space=pltpu.SMEM)


def partner_swap(block):
    return lax.ppermute(block, "sub", [(i, i ^ 1) for i in range(lax.axis_size("sub"))])


def stream(block, chips):
    count = lax.axis_size("sub")
    route = []
    for i in range(count):
        target = i + 2 * chips if i % 2 == 0 else i - 2 * chips
        route.append((i, target if 0 <= target < count else i ^ 1))
    return lax.ppermute(block, "sub", route)


def pick_kernel(place_ref, listed_ref, counts_ref, over_ref, swap_ref, keep_ref):
    me = place_ref[0]
    sign = place_ref[2]
    slots, tiles = over_ref.shape[0], over_ref.shape[1]

    def pick(k, out_ref, at):
        target = me + sign * k
        slot = jnp.int32(0)
        amount = jnp.int32(0)
        for n in range(slots):
            hit = listed_ref[n] == target
            slot = jnp.where(hit, n, slot)
            amount = jnp.where(hit, counts_ref[n], amount)
        for t in range(tiles):
            live = (t < amount).astype(jnp.bfloat16)
            out_ref[at, t] = over_ref[slot, t] * live

    for at, k in enumerate((1, -1, -2, -3, -4)):
        pick(k, swap_ref, at)
    for at, k in enumerate((2, 3, 4)):
        pick(k, keep_ref, at)


def gram_kernel(
    place_ref, rows_ref, own_ref, swap_ref, one_ref, two_ref, post_ref, matrix_ref,
    home_ref, ahead_ref, back_ref, left, right, acc,
):
    step = pl.program_id(0)
    vectors, width = own_ref.shape
    tiles, lanes = rows_ref.shape[1], rows_ref.shape[2]
    part = 256
    core, sign = place_ref[1], place_ref[2]

    def position(k):
        return jnp.where(core == 0, H + k, H + 1 - k)

    def right_rows(k):
        return pl.ds(pl.multiple_of(position(k) * vectors, vectors), vectors)

    @pl.when(step == 0)
    def _():
        left[0:vectors] = own_ref[...]
        right[right_rows(0)] = own_ref[...]
        right[right_rows(H + 1)] = jnp.zeros((vectors, width), jnp.bfloat16)
        sources = {
            1: (swap_ref, 0), 2: (post_ref, 1), 3: (post_ref, 0), 4: (post_ref, 2),
            -1: (one_ref, 1), -2: (one_ref, 0), -3: (two_ref, 1), -4: (two_ref, 0),
        }
        for at, k in enumerate(STACK):
            if k == 0:
                continue
            offset = sign * k
            slot = jnp.where(offset < 0, offset + H, offset + H - 1)
            source, which = sources[k]
            chosen = rows_ref[slot]
            low = chosen % part
            high = chosen // part
            index = lax.broadcasted_iota(jnp.int32, (part, lanes), 0)
            hot = jnp.concatenate(
                [
                    jnp.where(index == low[t : t + 1], 1.0, 0.0).astype(jnp.bfloat16)
                    for t in range(tiles)
                ],
                axis=1,
            )
            values = [source[which, t] for t in range(tiles)]
            spread = jnp.concatenate(
                [
                    jnp.concatenate(
                        [
                            values[t] * jnp.where(high[t : t + 1] == h, 1.0, 0.0).astype(jnp.bfloat16)
                            for t in range(tiles)
                        ],
                        axis=1,
                    )
                    for h in range(width // part)
                ],
                axis=0,
            )
            dense = lax.dot_general(
                spread, hot, (((1,), (1,)), ((), ())), preferred_element_type=jnp.float32
            ).astype(jnp.bfloat16)
            for h in range(width // part):
                block = dense[h * vectors : (h + 1) * vectors]
                left[at * vectors : (at + 1) * vectors, h * part : (h + 1) * part] = block
                right[right_rows(k), h * part : (h + 1) * part] = block

    product = jnp.dot(left[...], matrix_ref[...], preferred_element_type=jnp.float32).astype(
        jnp.bfloat16
    )
    columns = matrix_ref.shape[1]
    across = right[:, pl.ds(pl.multiple_of(step * columns, columns), columns)]
    term = lax.dot_general(
        product, across, (((1,), (1,)), ((), ())), preferred_element_type=jnp.float32
    )

    @pl.when(step == 0)
    def _():
        acc[...] = term

    @pl.when(step > 0)
    def _():
        acc[...] += term

    @pl.when(step == pl.num_programs(0) - 1)
    def _():
        for at in range(2):
            home_ref[at] = acc[at * vectors : (at + 1) * vectors]
        for at in range(3):
            ahead_ref[at] = acc[(2 + at) * vectors : (3 + at) * vectors]
        for at in range(4):
            back_ref[at] = acc[(5 + at) * vectors : (6 + at) * vectors].astype(jnp.bfloat16)


def window_kernel(place_ref, home_ref, one_ref, two_ref, near_ref, far_ref):
    core = place_ref[1]
    vectors = home_ref.shape[1]
    blocks = FULL

    def window(terms):
        total = None
        for value, start in terms:
            value = value.astype(jnp.float32)
            if start < 0:
                value = value[:, -start * vectors :]
                start = 0
            if start + value.shape[1] // vectors > blocks:
                value = value[:, : (blocks - start) * vectors]
            after = blocks * vectors - start * vectors - value.shape[1]
            value = jnp.pad(value, ((0, 0), (start * vectors, after)))
            total = value if total is None else total + value
        return total

    for c in range(2):
        way = 1 - 2 * c

        @pl.when(core == c)
        def _():
            for ref, at, row in ((near_ref, 0, c), (far_ref, 1, 1 - c)):
                ref[...] = window(
                    [
                        (home_ref[at], H - row),
                        (one_ref[at], H - 2 * way - row),
                        (two_ref[at], H - 4 * way - row),
                    ]
                )


def spread_kernel(place_ref, own_ref, up_ref, down_ref, far_ref, out_ref):
    x = place_ref[3]
    count = out_ref.shape[0]
    out_ref[x] = own_ref[...].astype(jnp.float32)
    out_ref[lax.rem(x + count - 1, count)] = up_ref[...].astype(jnp.float32)
    out_ref[lax.rem(x + 1, count)] = down_ref[...].astype(jnp.float32)
    out_ref[lax.rem(x + 2, count)] = far_ref[...].astype(jnp.float32)


def ring(block, distance):
    count = lax.axis_size("grp")
    return lax.ppermute(block, "grp", [(i, (i + distance) % count) for i in range(count)])


def on_device(blocks, own_vectors, over_vectors, neighbours, counts, margin_rows):
    device = lax.axis_index("sub")
    core = device % 2
    place = jnp.stack([device, core, 1 - 2 * core, lax.axis_index("grp")]).astype(jnp.int32)
    matrix = blocks[0, 0]
    width = matrix.shape[0]
    vectors = own_vectors.shape[2]
    over = over_vectors[0, 0]
    message = over.shape[1:]
    shape = jax.ShapeDtypeStruct

    give, keep = pl.pallas_call(
        pick_kernel,
        out_shape=(shape((5,) + message, jnp.bfloat16), shape((3,) + message, jnp.bfloat16)),
        in_specs=[SMEM, SMEM, SMEM, VMEM],
        out_specs=(VMEM, VMEM),
        name="pick",
    )(place, neighbours[0, 0], counts[0, 0], over)
    swap = partner_swap(give)
    two = stream(jnp.stack([keep[2], swap[3], swap[4]]), 2)
    one = stream(jnp.stack([keep[0], swap[1], keep[1], swap[2]]), 1)
    post = partner_swap(jnp.concatenate([one[2:4], two[2:3]]))

    columns = 256
    steps = width // columns
    whole = lambda *dims: pl.BlockSpec(dims, lambda i: (0,) * len(dims))
    home, ahead, back = pl.pallas_call(
        gram_kernel,
        grid=(steps,),
        out_shape=(
            shape((2, vectors, WIDE * vectors), jnp.float32),
            shape((3, vectors, WIDE * vectors), jnp.float32),
            shape((4, vectors, WIDE * vectors), jnp.bfloat16),
        ),
        in_specs=[
            SMEM,
            whole(*margin_rows.shape[2:]),
            whole(vectors, width),
            whole(*swap.shape),
            whole(*one.shape),
            whole(*two.shape),
            whole(*post.shape),
            pl.BlockSpec((width, columns), lambda i: (0, i)),
        ],
        out_specs=(
            whole(2, vectors, WIDE * vectors),
            whole(3, vectors, WIDE * vectors),
            whole(4, vectors, WIDE * vectors),
        ),
        scratch_shapes=[
            pltpu.VMEM((SPAN * vectors, width), jnp.bfloat16),
            pltpu.VMEM((WIDE * vectors, width), jnp.bfloat16),
            pltpu.VMEM((SPAN * vectors, WIDE * vectors), jnp.float32),
        ],
        compiler_params=pltpu.CompilerParams(vmem_limit_bytes=32 * 1024 * 1024),
        cost_estimate=pl.CostEstimate(flops=6 * 10**9, bytes_accessed=12 * 2**20, transcendentals=0),
        name="gram",
    )(place, margin_rows[0, 0], own_vectors[0, 0], swap, one, two, post, matrix)

    reverse = partner_swap(back).astype(jnp.float32)
    far_rows = stream(
        jnp.stack([ahead[2] + reverse[2], reverse[3]]).astype(jnp.bfloat16), 2
    )
    near_rows = stream((ahead[0:2] + reverse[0:2]).astype(jnp.bfloat16), 1)
    row = shape((vectors, FULL * vectors), jnp.float32)
    mine, other = pl.pallas_call(
        window_kernel,
        out_shape=(row, row),
        in_specs=[SMEM, VMEM, VMEM, VMEM],
        out_specs=(VMEM, VMEM),
        name="window",
    )(place, home, near_rows, far_rows)
    coarse = (mine + partner_swap(other)).astype(jnp.bfloat16)

    opposite = ring(coarse, 2)
    up = ring(coarse, 1)
    down = ring(coarse, -1)
    count = lax.axis_size("grp")
    spread = pl.pallas_call(
        spread_kernel,
        out_shape=shape((count, vectors, FULL * vectors), jnp.float32),
        in_specs=[SMEM, VMEM, VMEM, VMEM, VMEM],
        out_specs=VMEM,
        name="spread",
    )(place, coarse, up, down, opposite)
    return spread[:, None]


def solution(mesh):
    placed = (
        P("grp", "sub", None, None),
        P("grp", "sub", None, None),
        P("grp", "sub", None, None, None, None),
        P("grp", "sub", None),
        P("grp", "sub", None),
        P("grp", "sub", None, None, None),
    )
    return jax.shard_map(
        on_device, mesh=mesh, in_specs=placed, out_specs=P(None, "sub", None, None), check_vma=False
    )
```

```python
import jax
import jax.numpy as jnp
from jax import lax
from jax.experimental import pallas as pl
from jax.experimental.pallas import tpu as pltpu
from jax.sharding import PartitionSpec as P

H = 4
SPAN = 2 * H + 1
WIDE = SPAN + 1
FULL = 4 * H + 1
PART = 256
CHUNKS = 8
STACK = (0, 1, 2, 3, 4, -1, -2, -3, -4)
VMEM = pl.BlockSpec(memory_space=pltpu.VMEM)
HBM = pl.BlockSpec(memory_space=pltpu.HBM)


def partner_swap(block):
    return lax.ppermute(block, "sub", [(i, i ^ 1) for i in range(lax.axis_size("sub"))])


def stream(block, chips):
    count = lax.axis_size("sub")
    route = []
    for i in range(count):
        target = i + 2 * chips if i % 2 == 0 else i - 2 * chips
        route.append((i, target if 0 <= target < count else i ^ 1))
    return lax.ppermute(block, "sub", route)


def signs():
    me = lax.axis_index("sub")
    core = lax.rem(me, 2)
    return me, core, 1 - 2 * core


def pick_kernel(
    listed_hbm, counts_hbm, over_hbm, swap_ref, keep_ref, listed_ref, counts_ref, over_ref, sems
):
    pairs = [(listed_hbm, listed_ref), (counts_hbm, counts_ref)]
    pairs += [(over_hbm.at[n], over_ref.at[n]) for n in range(over_ref.shape[0])]
    copies = [
        pltpu.make_async_copy(source, target, sems.at[n])
        for n, (source, target) in enumerate(pairs)
    ]
    for copy in copies:
        copy.start()
    for copy in copies:
        copy.wait()
    me, core, sign = signs()
    slots, tiles = over_ref.shape[0], over_ref.shape[1]

    def pick(k, out_ref, at):
        target = me + sign * k
        slot = jnp.int32(0)
        amount = jnp.int32(0)
        for n in range(slots):
            hit = listed_ref[n] == target
            slot = jnp.where(hit, n, slot)
            amount = jnp.where(hit, counts_ref[n], amount)
        for t in range(tiles):
            live = (t < amount).astype(jnp.bfloat16)
            out_ref[at, t] = over_ref[slot, t] * live

    for at, k in enumerate((1, -1, -2, -3, -4)):
        pick(k, swap_ref, at)
    for at, k in enumerate((2, 3, 4)):
        pick(k, keep_ref, at)


def slot_of(sign, k):
    offset = sign * k
    return jnp.where(offset < 0, offset + H, offset + H - 1)


def expand(message, hot, mask):
    tiles, vectors, lanes = message.shape
    flat = jnp.concatenate([message[t] for t in range(tiles)], axis=1)
    parts = mask.shape[0]
    spread = jnp.concatenate([flat * mask[h : h + 1] for h in range(parts)], axis=0)
    dense = lax.dot_general(
        spread, hot, (((1,), (1,)), ((), ())), preferred_element_type=jnp.float32
    ).astype(jnp.bfloat16)
    return [dense[h * vectors : (h + 1) * vectors] for h in range(parts)]


def own_kernel(
    rows_hbm, own_hbm, matrix_hbm, swap_ref,
    matrix_ref, product_ref, present_ref, hot_ref, mask_ref, rows_ref, acc, sems, chunk_sems,
):
    width = matrix_ref.shape[0]
    vectors = own_hbm.shape[0]
    chunks = chunk_sems.shape[0]
    depth = width // chunks
    rows_copy = pltpu.make_async_copy(rows_hbm, rows_ref, sems.at[0])
    own_copy = pltpu.make_async_copy(own_hbm, present_ref.at[pl.ds(0, vectors)], sems.at[1])
    rows_copy.start()
    own_copy.start()
    copies = []
    for c in range(chunks):
        part = pl.ds(c * depth, depth)
        copy = pltpu.make_async_copy(matrix_hbm.at[part], matrix_ref.at[part], chunk_sems.at[c])
        copy.start()
        copies.append(copy)
    me, core, sign = signs()

    rows_copy.wait()
    lanes = rows_ref.shape[2]
    index = lax.broadcasted_iota(jnp.int32, (PART, lanes), 0)
    parts = lax.broadcasted_iota(jnp.int32, (width // PART, lanes), 0)
    for slot in range(rows_ref.shape[0]):
        low = rows_ref[slot] & (PART - 1)
        high = rows_ref[slot] // PART
        for t in range(rows_ref.shape[1]):
            place = slice(t * lanes, (t + 1) * lanes)
            hot_ref[slot, :, place] = jnp.where(index == low[t : t + 1], 1.0, 0.0).astype(jnp.bfloat16)
            mask_ref[slot, :, place] = jnp.where(parts == high[t : t + 1], 1.0, 0.0).astype(jnp.bfloat16)
    slot = slot_of(sign, 1)
    for h, block in enumerate(expand(swap_ref[0], hot_ref[slot], mask_ref[slot])):
        present_ref[vectors:, h * PART : (h + 1) * PART] = block

    own_copy.wait()
    for half in range(2):
        for copy in copies[half * chunks // 2 : (half + 1) * chunks // 2]:
            copy.wait()
        part = slice(half * width // 2, (half + 1) * width // 2)
        term = jnp.dot(
            present_ref[:, part], matrix_ref[part], preferred_element_type=jnp.float32
        )
        if half == 0:
            acc[...] = term
        else:
            product_ref[...] = (acc[...] + term).astype(jnp.bfloat16)


def near_kernel(matrix_ref, hot_ref, mask_ref, two_ref, one_ref, present_ref, product_ref):
    vectors = one_ref.shape[2]
    me, core, sign = signs()
    sources = (one_ref.at[1], one_ref.at[0], two_ref.at[1], two_ref.at[0])
    for at, source in enumerate(sources):
        slot = slot_of(sign, -1 - at)
        for h, block in enumerate(expand(source[...], hot_ref[slot], mask_ref[slot])):
            present_ref[at * vectors : (at + 1) * vectors, h * PART : (h + 1) * PART] = block
    product_ref[...] = jnp.dot(
        present_ref[...], matrix_ref[...], preferred_element_type=jnp.float32
    ).astype(jnp.bfloat16)


def times_all(product, right):
    return lax.dot_general(
        product, right, (((1,), (1,)), ((), ())), preferred_element_type=jnp.float32
    )


def back_kernel(
    own_present_ref, near_present_ref, near_product_ref, hot_ref, mask_ref, post_ref,
    far_present_ref, right_ref, back_ref,
):
    vectors = post_ref.shape[2]
    width = right_ref.shape[1]
    me, core, sign = signs()

    def right_rows(k):
        position = jnp.where(core == 0, H + k, H + 1 - k)
        return pl.ds(pl.multiple_of(position * vectors, vectors), vectors)

    right_ref[right_rows(H + 1)] = jnp.zeros((vectors, width), jnp.bfloat16)
    for at in range(2):
        right_ref[right_rows(at)] = own_present_ref[at * vectors : (at + 1) * vectors]
    for at in range(4):
        right_ref[right_rows(-1 - at)] = near_present_ref[at * vectors : (at + 1) * vectors]
    for at, source in enumerate((post_ref.at[2], post_ref.at[1], post_ref.at[0])):
        slot = slot_of(sign, 2 + at)
        for h, block in enumerate(expand(source[...], hot_ref[slot], mask_ref[slot])):
            place = slice(h * PART, (h + 1) * PART)
            far_present_ref[at * vectors : (at + 1) * vectors, place] = block
            right_ref[right_rows(2 + at), place] = block
    gram = times_all(near_product_ref[...], right_ref[...]).astype(jnp.bfloat16)
    for at in range(4):
        back_ref[at] = gram[at * vectors : (at + 1) * vectors]


def ahead_kernel(
    matrix_ref, own_product_ref, far_present_ref, right_ref, home_ref, ahead_ref, product
):
    vectors = home_ref.shape[1]
    product[0 : 2 * vectors] = own_product_ref[...]
    product[2 * vectors :] = jnp.dot(
        far_present_ref[...], matrix_ref[...], preferred_element_type=jnp.float32
    ).astype(jnp.bfloat16)
    gram = times_all(product[...], right_ref[...])
    for at in range(2):
        home_ref[at] = gram[at * vectors : (at + 1) * vectors]
    for at in range(3):
        ahead_ref[at] = gram[(2 + at) * vectors : (3 + at) * vectors]


def window_kernel(home_ref, one_ref, two_ref, near_ref, far_ref):
    me, core, sign = signs()
    vectors = home_ref.shape[1]
    blocks = FULL

    def window(terms):
        total = None
        for value, start in terms:
            value = value.astype(jnp.float32)
            if start < 0:
                value = value[:, -start * vectors :]
                start = 0
            if start + value.shape[1] // vectors > blocks:
                value = value[:, : (blocks - start) * vectors]
            after = blocks * vectors - start * vectors - value.shape[1]
            value = jnp.pad(value, ((0, 0), (start * vectors, after)))
            total = value if total is None else total + value
        return total

    for c in range(2):
        way = 1 - 2 * c

        @pl.when(core == c)
        def _():
            for ref, at, row in ((near_ref, 0, c), (far_ref, 1, 1 - c)):
                ref[...] = window(
                    [
                        (home_ref[at], H - row),
                        (one_ref[at], H - 2 * way - row),
                        (two_ref[at], H - 4 * way - row),
                    ]
                )


def spread_kernel(own_ref, one_ref, three_ref, two_ref, out_hbm, wide, sems):
    x = lax.axis_index("grp")
    copies = []
    for d, ref in enumerate((own_ref, one_ref, two_ref, three_ref)):
        wide[d] = ref[...].astype(jnp.float32)
        copy = pltpu.make_async_copy(wide.at[d], out_hbm.at[x ^ d], sems.at[d])
        copy.start()
        copies.append(copy)
    for copy in copies:
        copy.wait()


def across(block, bits):
    return lax.ppermute(block, "grp", [(i, i ^ bits) for i in range(lax.axis_size("grp"))])


def limit(mib):
    return pltpu.CompilerParams(vmem_limit_bytes=mib * 2**20)


def in_hbm(array):
    return pltpu.with_memory_space_constraint(array, pltpu.HBM)


def on_device(blocks, own_vectors, over_vectors, neighbours, counts, margin_rows):
    matrix = blocks[0, 0]
    width = matrix.shape[0]
    vectors = own_vectors.shape[2]
    over, rows = over_vectors[0, 0], margin_rows[0, 0]
    message = over.shape[1:]
    f32, bf16 = jnp.float32, jnp.bfloat16

    give, keep = pl.pallas_call(
        pick_kernel,
        out_shape=(pltpu.VMEM((5,) + message, bf16), pltpu.VMEM((3,) + message, bf16)),
        in_specs=[HBM] * 3,
        out_specs=(VMEM, VMEM),
        scratch_shapes=[
            pltpu.SMEM(neighbours.shape[2:], jnp.int32),
            pltpu.SMEM(counts.shape[2:], jnp.int32),
            pltpu.VMEM(over.shape, bf16),
            pltpu.SemaphoreType.DMA((2 + over.shape[0],)),
        ],
        compiler_params=limit(6),
        name="pick",
    )(in_hbm(neighbours[0, 0]), in_hbm(counts[0, 0]), in_hbm(over))
    swap = partner_swap(give)
    two = stream(jnp.stack([keep[2], swap[3], swap[4]]), 2)
    one = stream(jnp.stack([keep[0], swap[1], keep[1], swap[2]]), 1)

    loaded, own_product, own_present, hot, mask = pl.pallas_call(
        own_kernel,
        out_shape=(
            pltpu.VMEM((width, width), bf16),
            pltpu.VMEM((2 * vectors, width), bf16),
            pltpu.VMEM((2 * vectors, width), bf16),
            pltpu.VMEM((rows.shape[0], PART, rows.shape[1] * rows.shape[2]), bf16),
            pltpu.VMEM((rows.shape[0], width // PART, rows.shape[1] * rows.shape[2]), bf16),
        ),
        in_specs=[HBM, HBM, HBM, VMEM],
        out_specs=(VMEM,) * 5,
        scratch_shapes=[
            pltpu.VMEM(rows.shape, jnp.int32),
            pltpu.VMEM((2 * vectors, width), f32),
            pltpu.SemaphoreType.DMA((2,)),
            pltpu.SemaphoreType.DMA((CHUNKS,)),
        ],
        compiler_params=limit(16),
        cost_estimate=pl.CostEstimate(flops=10**9, bytes_accessed=10 * 2**20, transcendentals=0),
        name="own",
    )(in_hbm(rows), in_hbm(own_vectors[0, 0]), in_hbm(matrix), swap)

    two, one, mask = lax.optimization_barrier((two, one, mask))
    post = partner_swap(jnp.concatenate([two[2:3], one[2:4]]))

    near_present, near_product = pl.pallas_call(
        near_kernel,
        out_shape=(pltpu.VMEM((4 * vectors, width), bf16),) * 2,
        in_specs=[VMEM] * 5,
        out_specs=(VMEM,) * 2,
        compiler_params=limit(12),
        cost_estimate=pl.CostEstimate(flops=2 * 10**9, bytes_accessed=2**20, transcendentals=0),
        name="near",
    )(loaded, hot, mask, two, one)
    post, near_product = lax.optimization_barrier((post, near_product))
    far_present, right, back = pl.pallas_call(
        back_kernel,
        out_shape=(
            pltpu.VMEM((3 * vectors, width), bf16),
            pltpu.VMEM((WIDE * vectors, width), bf16),
            pltpu.VMEM((4, vectors, WIDE * vectors), bf16),
        ),
        in_specs=[VMEM] * 6,
        out_specs=(VMEM,) * 3,
        compiler_params=limit(12),
        cost_estimate=pl.CostEstimate(flops=10**9, bytes_accessed=2**20, transcendentals=0),
        name="back",
    )(own_present, near_present, near_product, hot, mask, post)
    reverse = partner_swap(back)
    home, ahead = pl.pallas_call(
        ahead_kernel,
        out_shape=(
            pltpu.VMEM((2, vectors, WIDE * vectors), f32),
            pltpu.VMEM((3, vectors, WIDE * vectors), f32),
        ),
        in_specs=[VMEM] * 4,
        out_specs=(VMEM,) * 2,
        scratch_shapes=[pltpu.VMEM((5 * vectors, width), bf16)],
        compiler_params=limit(12),
        cost_estimate=pl.CostEstimate(flops=2 * 10**9, bytes_accessed=2**20, transcendentals=0),
        name="ahead",
    )(loaded, own_product, far_present, right)
    reverse, ahead = lax.optimization_barrier((reverse, ahead))
    reverse = reverse.astype(f32)

    far_rows = stream(
        jnp.stack([ahead[2] + reverse[2], reverse[3]]).astype(jnp.bfloat16), 2
    )
    near_rows = stream((ahead[0:2] + reverse[0:2]).astype(jnp.bfloat16), 1)
    row = pltpu.VMEM((vectors, FULL * vectors), f32)
    mine, other = pl.pallas_call(
        window_kernel,
        out_shape=(row, row),
        in_specs=[VMEM, VMEM, VMEM],
        out_specs=(VMEM, VMEM),
        compiler_params=limit(6),
        name="window",
    )(home, near_rows, far_rows)
    coarse = (mine + partner_swap(other)).astype(jnp.bfloat16)

    across_two = across(coarse, 2)
    across_three = across(coarse, 3)
    across_one = across(coarse, 1)
    count = lax.axis_size("grp")
    gathered = pl.pallas_call(
        spread_kernel,
        out_shape=pltpu.HBM((count,) + row.shape, f32),
        in_specs=[VMEM] * 4,
        out_specs=HBM,
        scratch_shapes=[
            pltpu.VMEM((count,) + row.shape, f32),
            pltpu.SemaphoreType.DMA((count,)),
        ],
        compiler_params=limit(6),
        name="spread",
    )(coarse, across_one, across_three, across_two)
    return gathered[:, None]


def solution(mesh):
    placed = (
        P("grp", "sub", None, None),
        P("grp", "sub", None, None),
        P("grp", "sub", None, None, None, None),
        P("grp", "sub", None),
        P("grp", "sub", None),
        P("grp", "sub", None, None, None),
    )
    return jax.shard_map(
        on_device, mesh=mesh, in_specs=placed, out_specs=P(None, "sub", None, None), check_vma=False
    )
```

```python
import jax
import jax.numpy as jnp
from jax import lax
from jax.experimental import pallas as pl
from jax.experimental.pallas import tpu as pltpu
from jax.sharding import PartitionSpec as P

H = 4
SPAN = 2 * H + 1
WIDE = SPAN + 1
FULL = 4 * H + 1
PART = 256
STACK = (0, 1, 2, 3, 4, -1, -2, -3, -4)
VMEM = pl.BlockSpec(memory_space=pltpu.VMEM)
HBM = pl.BlockSpec(memory_space=pltpu.HBM)


def partner_swap(block):
    return lax.ppermute(block, "sub", [(i, i ^ 1) for i in range(lax.axis_size("sub"))])


def stream(block, chips):
    count = lax.axis_size("sub")
    route = []
    for i in range(count):
        target = i + 2 * chips if i % 2 == 0 else i - 2 * chips
        route.append((i, target if 0 <= target < count else i ^ 1))
    return lax.ppermute(block, "sub", route)


def signs():
    me = lax.axis_index("sub")
    core = lax.rem(me, 2)
    return me, core, 1 - 2 * core


def pick_kernel(
    listed_hbm, counts_hbm, over_hbm, swap_ref, keep_ref, listed_ref, counts_ref, over_ref, sems
):
    pairs = [(listed_hbm, listed_ref), (counts_hbm, counts_ref)]
    pairs += [(over_hbm.at[n], over_ref.at[n]) for n in range(over_ref.shape[0])]
    copies = [
        pltpu.make_async_copy(source, target, sems.at[n])
        for n, (source, target) in enumerate(pairs)
    ]
    for copy in copies:
        copy.start()
    for copy in copies:
        copy.wait()
    me, core, sign = signs()
    slots, tiles = over_ref.shape[0], over_ref.shape[1]

    def pick(k, out_ref, at):
        target = me + sign * k
        slot = jnp.int32(0)
        amount = jnp.int32(0)
        for n in range(slots):
            hit = listed_ref[n] == target
            slot = jnp.where(hit, n, slot)
            amount = jnp.where(hit, counts_ref[n], amount)
        for t in range(tiles):
            live = (t < amount).astype(jnp.bfloat16)
            out_ref[at, t] = over_ref[slot, t] * live

    for at, k in enumerate((1, -1, -2, -3, -4)):
        pick(k, swap_ref, at)
    for at, k in enumerate((2, 3, 4)):
        pick(k, keep_ref, at)


def slot_of(sign, k):
    offset = sign * k
    return jnp.where(offset < 0, offset + H, offset + H - 1)


def expand(message, hot, mask):
    tiles, vectors, lanes = message.shape
    flat = jnp.concatenate([message[t] for t in range(tiles)], axis=1)
    parts = mask.shape[0]
    spread = jnp.concatenate([flat * mask[h : h + 1] for h in range(parts)], axis=0)
    dense = lax.dot_general(
        spread, hot, (((1,), (1,)), ((), ())), preferred_element_type=jnp.float32
    ).astype(jnp.bfloat16)
    return [dense[h * vectors : (h + 1) * vectors] for h in range(parts)]


def hot_kernel(rows_hbm, hot_ref, mask_ref, rows_ref, sem):
    copy = pltpu.make_async_copy(rows_hbm, rows_ref, sem)
    copy.start()
    copy.wait()
    lanes = rows_ref.shape[2]
    index = lax.broadcasted_iota(jnp.int32, (PART, lanes), 0)
    parts = lax.broadcasted_iota(jnp.int32, (mask_ref.shape[1], lanes), 0)
    for slot in range(rows_ref.shape[0]):
        low = rows_ref[slot] & (PART - 1)
        high = rows_ref[slot] // PART
        for t in range(rows_ref.shape[1]):
            place = slice(t * lanes, (t + 1) * lanes)
            hot_ref[slot, :, place] = jnp.where(index == low[t : t + 1], 1.0, 0.0).astype(jnp.bfloat16)
            mask_ref[slot, :, place] = jnp.where(parts == high[t : t + 1], 1.0, 0.0).astype(jnp.bfloat16)


def own_kernel(own_hbm, swap_ref, hot_ref, mask_ref, present_ref, sem):
    vectors = own_hbm.shape[0]
    own_copy = pltpu.make_async_copy(own_hbm, present_ref.at[pl.ds(0, vectors)], sem)
    own_copy.start()
    me, core, sign = signs()
    slot = slot_of(sign, 1)
    for h, block in enumerate(expand(swap_ref[0], hot_ref[slot], mask_ref[slot])):
        present_ref[vectors:, h * PART : (h + 1) * PART] = block
    own_copy.wait()


def times_kernel(present_ref, matrix_ref, product_ref):
    product_ref[...] = jnp.dot(
        present_ref[...], matrix_ref[...], preferred_element_type=jnp.float32
    ).astype(jnp.bfloat16)


def pair_kernel(hot_ref, mask_ref, two_ref, present_ref):
    vectors = two_ref.shape[2]
    me, core, sign = signs()
    for at, source in enumerate((two_ref.at[1], two_ref.at[0])):
        slot = slot_of(sign, -3 - at)
        for h, block in enumerate(expand(source[...], hot_ref[slot], mask_ref[slot])):
            present_ref[at * vectors : (at + 1) * vectors, h * PART : (h + 1) * PART] = block


def near_kernel(matrix_ref, hot_ref, mask_ref, pair_ref, one_ref, present_ref, product_ref):
    vectors = one_ref.shape[2]
    me, core, sign = signs()
    present_ref[2 * vectors :] = pair_ref[...]
    for at, source in enumerate((one_ref.at[1], one_ref.at[0])):
        slot = slot_of(sign, -1 - at)
        for h, block in enumerate(expand(source[...], hot_ref[slot], mask_ref[slot])):
            present_ref[at * vectors : (at + 1) * vectors, h * PART : (h + 1) * PART] = block
    product_ref[...] = jnp.dot(
        present_ref[...], matrix_ref[...], preferred_element_type=jnp.float32
    ).astype(jnp.bfloat16)


def times_all(product, right):
    return lax.dot_general(
        product, right, (((1,), (1,)), ((), ())), preferred_element_type=jnp.float32
    )


def back_kernel(
    own_present_ref, near_present_ref, near_product_ref, hot_ref, mask_ref, post_ref,
    far_present_ref, right_ref, back_ref,
):
    vectors = post_ref.shape[2]
    width = right_ref.shape[1]
    me, core, sign = signs()

    def right_rows(k):
        position = jnp.where(core == 0, H + k, H + 1 - k)
        return pl.ds(pl.multiple_of(position * vectors, vectors), vectors)

    right_ref[right_rows(H + 1)] = jnp.zeros((vectors, width), jnp.bfloat16)
    for at in range(2):
        right_ref[right_rows(at)] = own_present_ref[at * vectors : (at + 1) * vectors]
    for at in range(4):
        right_ref[right_rows(-1 - at)] = near_present_ref[at * vectors : (at + 1) * vectors]
    for at, source in enumerate((post_ref.at[2], post_ref.at[1], post_ref.at[0])):
        slot = slot_of(sign, 2 + at)
        for h, block in enumerate(expand(source[...], hot_ref[slot], mask_ref[slot])):
            place = slice(h * PART, (h + 1) * PART)
            far_present_ref[at * vectors : (at + 1) * vectors, place] = block
            right_ref[right_rows(2 + at), place] = block
    gram = times_all(near_product_ref[...], right_ref[...]).astype(jnp.bfloat16)
    for at in range(4):
        back_ref[at] = gram[at * vectors : (at + 1) * vectors]


def ahead_kernel(
    matrix_ref, own_product_ref, far_present_ref, right_ref, home_ref, ahead_ref, product
):
    vectors = home_ref.shape[1]
    product[0 : 2 * vectors] = own_product_ref[...]
    product[2 * vectors :] = jnp.dot(
        far_present_ref[...], matrix_ref[...], preferred_element_type=jnp.float32
    ).astype(jnp.bfloat16)
    gram = times_all(product[...], right_ref[...])
    for at in range(2):
        home_ref[at] = gram[at * vectors : (at + 1) * vectors]
    for at in range(3):
        ahead_ref[at] = gram[(2 + at) * vectors : (3 + at) * vectors]


def window_kernel(home_ref, one_ref, two_ref, near_ref, far_ref):
    me, core, sign = signs()
    vectors = home_ref.shape[1]
    blocks = FULL

    def window(terms):
        total = None
        for value, start in terms:
            value = value.astype(jnp.float32)
            if start < 0:
                value = value[:, -start * vectors :]
                start = 0
            if start + value.shape[1] // vectors > blocks:
                value = value[:, : (blocks - start) * vectors]
            after = blocks * vectors - start * vectors - value.shape[1]
            value = jnp.pad(value, ((0, 0), (start * vectors, after)))
            total = value if total is None else total + value
        return total

    for c in range(2):
        way = 1 - 2 * c

        @pl.when(core == c)
        def _():
            for ref, at, row in ((near_ref, 0, c), (far_ref, 1, 1 - c)):
                ref[...] = window(
                    [
                        (home_ref[at], H - row),
                        (one_ref[at], H - 2 * way - row),
                        (two_ref[at], H - 4 * way - row),
                    ]
                )


def spread_kernel(own_ref, one_ref, three_ref, two_ref, out_hbm, wide, sems):
    x = lax.axis_index("grp")
    copies = []
    for d, ref in enumerate((own_ref, one_ref, two_ref, three_ref)):
        wide[d] = ref[...].astype(jnp.float32)
        copy = pltpu.make_async_copy(wide.at[d], out_hbm.at[x ^ d], sems.at[d])
        copy.start()
        copies.append(copy)
    for copy in copies:
        copy.wait()


def across(block, bits):
    return lax.ppermute(block, "grp", [(i, i ^ bits) for i in range(lax.axis_size("grp"))])


def limit(mib):
    return pltpu.CompilerParams(vmem_limit_bytes=mib * 2**20)


def in_hbm(array):
    return pltpu.with_memory_space_constraint(array, pltpu.HBM)


def on_device(blocks, own_vectors, over_vectors, neighbours, counts, margin_rows):
    matrix = blocks[0, 0]
    width = matrix.shape[0]
    vectors = own_vectors.shape[2]
    over, rows = over_vectors[0, 0], margin_rows[0, 0]
    message = over.shape[1:]
    f32, bf16 = jnp.float32, jnp.bfloat16

    give, keep = pl.pallas_call(
        pick_kernel,
        out_shape=(pltpu.VMEM((5,) + message, bf16), pltpu.VMEM((3,) + message, bf16)),
        in_specs=[HBM] * 3,
        out_specs=(VMEM, VMEM),
        scratch_shapes=[
            pltpu.SMEM(neighbours.shape[2:], jnp.int32),
            pltpu.SMEM(counts.shape[2:], jnp.int32),
            pltpu.VMEM(over.shape, bf16),
            pltpu.SemaphoreType.DMA((2 + over.shape[0],)),
        ],
        compiler_params=limit(6),
        name="pick",
    )(in_hbm(neighbours[0, 0]), in_hbm(counts[0, 0]), in_hbm(over))
    swap = partner_swap(give)
    size = rows.shape[1] * rows.shape[2]
    hot, mask = pl.pallas_call(
        hot_kernel,
        out_shape=(
            pltpu.VMEM((rows.shape[0], PART, size), bf16),
            pltpu.VMEM((rows.shape[0], width // PART, size), bf16),
        ),
        in_specs=[HBM],
        out_specs=(VMEM,) * 2,
        scratch_shapes=[pltpu.VMEM(rows.shape, jnp.int32), pltpu.SemaphoreType.DMA],
        compiler_params=limit(4),
        cost_estimate=pl.CostEstimate(flops=10**9, bytes_accessed=2**24, transcendentals=0),
        name="hot",
    )(in_hbm(rows))
    swap, mask = lax.optimization_barrier((swap, mask))
    two = stream(jnp.stack([keep[2], swap[3], swap[4]]), 2)
    one = stream(jnp.stack([keep[0], swap[1], keep[1], swap[2]]), 1)

    own_present = pl.pallas_call(
        own_kernel,
        out_shape=pltpu.VMEM((2 * vectors, width), bf16),
        in_specs=[HBM, VMEM, VMEM, VMEM],
        out_specs=VMEM,
        scratch_shapes=[pltpu.SemaphoreType.DMA],
        compiler_params=limit(8),
        cost_estimate=pl.CostEstimate(flops=10**9, bytes_accessed=2**24, transcendentals=0),
        name="own",
    )(in_hbm(own_vectors[0, 0]), swap, hot, mask)
    loaded = pltpu.with_memory_space_constraint(matrix, pltpu.VMEM)
    own_product = pl.pallas_call(
        times_kernel,
        out_shape=pltpu.VMEM((2 * vectors, width), bf16),
        in_specs=[VMEM, VMEM],
        out_specs=VMEM,
        compiler_params=limit(8),
        cost_estimate=pl.CostEstimate(flops=10**9, bytes_accessed=2**23, transcendentals=0),
        name="times",
    )(own_present, loaded)
    two, own_product = lax.optimization_barrier((two, own_product))
    pair = pl.pallas_call(
        pair_kernel,
        out_shape=pltpu.VMEM((2 * vectors, width), bf16),
        in_specs=[VMEM] * 3,
        out_specs=VMEM,
        compiler_params=limit(8),
        cost_estimate=pl.CostEstimate(flops=10**9, bytes_accessed=2**23, transcendentals=0),
        name="pair",
    )(hot, mask, two)
    one, pair = lax.optimization_barrier((one, pair))
    post = partner_swap(jnp.concatenate([two[2:3], one[2:4]]))

    near_present, near_product = pl.pallas_call(
        near_kernel,
        out_shape=(pltpu.VMEM((4 * vectors, width), bf16),) * 2,
        in_specs=[VMEM] * 5,
        out_specs=(VMEM,) * 2,
        compiler_params=limit(12),
        cost_estimate=pl.CostEstimate(flops=2 * 10**9, bytes_accessed=2**20, transcendentals=0),
        name="near",
    )(loaded, hot, mask, pair, one)
    post, near_product = lax.optimization_barrier((post, near_product))
    far_present, right, back = pl.pallas_call(
        back_kernel,
        out_shape=(
            pltpu.VMEM((3 * vectors, width), bf16),
            pltpu.VMEM((WIDE * vectors, width), bf16),
            pltpu.VMEM((4, vectors, WIDE * vectors), bf16),
        ),
        in_specs=[VMEM] * 6,
        out_specs=(VMEM,) * 3,
        compiler_params=limit(12),
        cost_estimate=pl.CostEstimate(flops=10**9, bytes_accessed=2**20, transcendentals=0),
        name="back",
    )(own_present, near_present, near_product, hot, mask, post)
    reverse = partner_swap(back)
    home, ahead = pl.pallas_call(
        ahead_kernel,
        out_shape=(
            pltpu.VMEM((2, vectors, WIDE * vectors), f32),
            pltpu.VMEM((3, vectors, WIDE * vectors), f32),
        ),
        in_specs=[VMEM] * 4,
        out_specs=(VMEM,) * 2,
        scratch_shapes=[pltpu.VMEM((5 * vectors, width), bf16)],
        compiler_params=limit(12),
        cost_estimate=pl.CostEstimate(flops=2 * 10**9, bytes_accessed=2**20, transcendentals=0),
        name="ahead",
    )(loaded, own_product, far_present, right)
    reverse, ahead = lax.optimization_barrier((reverse, ahead))
    reverse = reverse.astype(f32)

    far_rows = stream(
        jnp.stack([ahead[2] + reverse[2], reverse[3]]).astype(jnp.bfloat16), 2
    )
    near_rows = stream((ahead[0:2] + reverse[0:2]).astype(jnp.bfloat16), 1)
    row = pltpu.VMEM((vectors, FULL * vectors), f32)
    mine, other = pl.pallas_call(
        window_kernel,
        out_shape=(row, row),
        in_specs=[VMEM, VMEM, VMEM],
        out_specs=(VMEM, VMEM),
        compiler_params=limit(6),
        name="window",
    )(home, near_rows, far_rows)
    coarse = (mine + partner_swap(other)).astype(jnp.bfloat16)

    across_two = across(coarse, 2)
    across_three = across(coarse, 3)
    across_one = across(coarse, 1)
    count = lax.axis_size("grp")
    gathered = pl.pallas_call(
        spread_kernel,
        out_shape=pltpu.HBM((count,) + row.shape, f32),
        in_specs=[VMEM] * 4,
        out_specs=HBM,
        scratch_shapes=[
            pltpu.VMEM((count,) + row.shape, f32),
            pltpu.SemaphoreType.DMA((count,)),
        ],
        compiler_params=limit(6),
        name="spread",
    )(coarse, across_one, across_three, across_two)
    return gathered[:, None]


def solution(mesh):
    placed = (
        P("grp", "sub", None, None),
        P("grp", "sub", None, None),
        P("grp", "sub", None, None, None, None),
        P("grp", "sub", None),
        P("grp", "sub", None),
        P("grp", "sub", None, None, None),
    )
    return jax.shard_map(
        on_device, mesh=mesh, in_specs=placed, out_specs=P(None, "sub", None, None), check_vma=False
    )
```

```python
import jax
import jax.numpy as jnp
from jax import lax
from jax.experimental import pallas as pl
from jax.experimental.pallas import tpu as pltpu
from jax.sharding import PartitionSpec as P

H = 4
SPAN = 2 * H + 1
WIDE = SPAN + 1
FULL = 4 * H + 1
PART = 256
STACK = (0, 1, 2, 3, 4, -1, -2, -3, -4)
VMEM = pl.BlockSpec(memory_space=pltpu.VMEM)
HBM = pl.BlockSpec(memory_space=pltpu.HBM)


def partner_swap(block):
    return lax.ppermute(block, "sub", [(i, i ^ 1) for i in range(lax.axis_size("sub"))])


def stream(block, chips):
    count = lax.axis_size("sub")
    route = []
    for i in range(count):
        target = i + 2 * chips if i % 2 == 0 else i - 2 * chips
        route.append((i, target if 0 <= target < count else i ^ 1))
    return lax.ppermute(block, "sub", route)


def signs():
    me = lax.axis_index("sub")
    core = lax.rem(me, 2)
    return me, core, 1 - 2 * core


def pick_kernel(
    listed_hbm, counts_hbm, over_hbm, swap_ref, keep_ref, listed_ref, counts_ref, over_ref, sems
):
    pairs = [(listed_hbm, listed_ref), (counts_hbm, counts_ref)]
    pairs += [(over_hbm.at[n], over_ref.at[n]) for n in range(over_ref.shape[0])]
    copies = [
        pltpu.make_async_copy(source, target, sems.at[n])
        for n, (source, target) in enumerate(pairs)
    ]
    for copy in copies:
        copy.start()
    for copy in copies:
        copy.wait()
    me, core, sign = signs()
    slots, tiles = over_ref.shape[0], over_ref.shape[1]

    def pick(k, out_ref, at):
        target = me + sign * k
        slot = jnp.int32(0)
        amount = jnp.int32(0)
        for n in range(slots):
            hit = listed_ref[n] == target
            slot = jnp.where(hit, n, slot)
            amount = jnp.where(hit, counts_ref[n], amount)
        for t in range(tiles):
            live = (t < amount).astype(jnp.bfloat16)
            out_ref[at, t] = over_ref[slot, t] * live

    for at, k in enumerate((1, -1, -2, -3, -4)):
        pick(k, swap_ref, at)
    for at, k in enumerate((2, 3, 4)):
        pick(k, keep_ref, at)


def slot_of(sign, k):
    offset = sign * k
    return jnp.where(offset < 0, offset + H, offset + H - 1)


def expand(message, hot, mask):
    tiles, vectors, lanes = message.shape
    flat = jnp.concatenate([message[t] for t in range(tiles)], axis=1)
    parts = mask.shape[0]
    spread = jnp.concatenate(
        [flat * mask[h : h + 1].astype(jnp.bfloat16) for h in range(parts)], axis=0
    )
    dense = lax.dot_general(
        spread, hot, (((1,), (1,)), ((), ())), preferred_element_type=jnp.float32
    ).astype(jnp.bfloat16)
    return [dense[h * vectors : (h + 1) * vectors] for h in range(parts)]


def hot_kernel(rows_hbm, hot_ref, mask_ref, rows_ref, sem):
    copy = pltpu.make_async_copy(rows_hbm, rows_ref, sem)
    copy.start()
    copy.wait()
    lanes = rows_ref.shape[2]
    index = lax.broadcasted_iota(jnp.int32, (PART, lanes), 0)
    parts = lax.broadcasted_iota(jnp.int32, (mask_ref.shape[1], lanes), 0)
    for slot in range(rows_ref.shape[0]):
        low = rows_ref[slot] & (PART - 1)
        high = rows_ref[slot] // PART
        for t in range(rows_ref.shape[1]):
            place = slice(t * lanes, (t + 1) * lanes)
            hot_ref[slot, :, place] = jnp.where(index == low[t : t + 1], 1.0, 0.0).astype(jnp.bfloat16)
            mask_ref[slot, :, place] = jnp.where(parts == high[t : t + 1], 1.0, 0.0)


def own_kernel(own_hbm, swap_ref, hot_ref, mask_ref, present_ref, sem):
    vectors = own_hbm.shape[0]
    own_copy = pltpu.make_async_copy(own_hbm, present_ref.at[pl.ds(0, vectors)], sem)
    own_copy.start()
    me, core, sign = signs()
    slot = slot_of(sign, 1)
    for h, block in enumerate(expand(swap_ref[0], hot_ref[slot], mask_ref[slot])):
        present_ref[vectors:, h * PART : (h + 1) * PART] = block
    own_copy.wait()


def times_kernel(present_ref, matrix_ref, product_ref):
    product_ref[...] = jnp.dot(
        present_ref[...], matrix_ref[...], preferred_element_type=jnp.float32
    ).astype(jnp.bfloat16)


def pair_kernel(hot_ref, mask_ref, two_ref, present_ref):
    vectors = two_ref.shape[2]
    me, core, sign = signs()
    for at, source in enumerate((two_ref.at[1], two_ref.at[0])):
        slot = slot_of(sign, -3 - at)
        for h, block in enumerate(expand(source[...], hot_ref[slot], mask_ref[slot])):
            present_ref[at * vectors : (at + 1) * vectors, h * PART : (h + 1) * PART] = block


def near_kernel(matrix_ref, hot_ref, mask_ref, pair_ref, one_ref, present_ref, product_ref):
    vectors = one_ref.shape[2]
    me, core, sign = signs()
    present_ref[2 * vectors :] = pair_ref[...]
    for at, source in enumerate((one_ref.at[1], one_ref.at[0])):
        slot = slot_of(sign, -1 - at)
        for h, block in enumerate(expand(source[...], hot_ref[slot], mask_ref[slot])):
            present_ref[at * vectors : (at + 1) * vectors, h * PART : (h + 1) * PART] = block
    product_ref[...] = jnp.dot(
        present_ref[...], matrix_ref[...], preferred_element_type=jnp.float32
    ).astype(jnp.bfloat16)


def times_all(product, right):
    return lax.dot_general(
        product, right, (((1,), (1,)), ((), ())), preferred_element_type=jnp.float32
    )


def back_kernel(
    own_present_ref, near_present_ref, near_product_ref, hot_ref, mask_ref, post_ref,
    far_present_ref, right_ref, back_ref,
):
    vectors = post_ref.shape[2]
    width = right_ref.shape[1]
    me, core, sign = signs()

    def right_rows(k):
        position = jnp.where(core == 0, H + k, H + 1 - k)
        return pl.ds(pl.multiple_of(position * vectors, vectors), vectors)

    right_ref[right_rows(H + 1)] = jnp.zeros((vectors, width), jnp.bfloat16)
    for at in range(2):
        right_ref[right_rows(at)] = own_present_ref[at * vectors : (at + 1) * vectors]
    for at in range(4):
        right_ref[right_rows(-1 - at)] = near_present_ref[at * vectors : (at + 1) * vectors]
    for at, source in enumerate((post_ref.at[2], post_ref.at[1], post_ref.at[0])):
        slot = slot_of(sign, 2 + at)
        for h, block in enumerate(expand(source[...], hot_ref[slot], mask_ref[slot])):
            place = slice(h * PART, (h + 1) * PART)
            far_present_ref[at * vectors : (at + 1) * vectors, place] = block
            right_ref[right_rows(2 + at), place] = block
    gram = times_all(near_product_ref[...], right_ref[...]).astype(jnp.bfloat16)
    for at in range(4):
        back_ref[at] = gram[at * vectors : (at + 1) * vectors]


def ahead_kernel(
    matrix_ref, own_product_ref, far_present_ref, right_ref, home_ref, ahead_ref, product
):
    vectors = home_ref.shape[1]
    product[0 : 2 * vectors] = own_product_ref[...]
    product[2 * vectors :] = jnp.dot(
        far_present_ref[...], matrix_ref[...], preferred_element_type=jnp.float32
    ).astype(jnp.bfloat16)
    gram = times_all(product[...], right_ref[...])
    for at in range(2):
        home_ref[at] = gram[at * vectors : (at + 1) * vectors]
    for at in range(3):
        ahead_ref[at] = gram[(2 + at) * vectors : (3 + at) * vectors]


def window_kernel(home_ref, one_ref, two_ref, near_ref, far_ref):
    me, core, sign = signs()
    vectors = home_ref.shape[1]
    blocks = FULL

    def window(terms):
        total = None
        for value, start in terms:
            value = value.astype(jnp.float32)
            if start < 0:
                value = value[:, -start * vectors :]
                start = 0
            if start + value.shape[1] // vectors > blocks:
                value = value[:, : (blocks - start) * vectors]
            after = blocks * vectors - start * vectors - value.shape[1]
            value = jnp.pad(value, ((0, 0), (start * vectors, after)))
            total = value if total is None else total + value
        return total

    for c in range(2):
        way = 1 - 2 * c

        @pl.when(core == c)
        def _():
            for ref, at, row in ((near_ref, 0, c), (far_ref, 1, 1 - c)):
                ref[...] = window(
                    [
                        (home_ref[at], H - row),
                        (one_ref[at], H - 2 * way - row),
                        (two_ref[at], H - 4 * way - row),
                    ]
                )


def spread_kernel(own_ref, one_ref, three_ref, two_ref, out_hbm, wide, sems):
    x = lax.axis_index("grp")
    copies = []
    for d, ref in enumerate((own_ref, one_ref, two_ref, three_ref)):
        wide[d] = ref[...].astype(jnp.float32)
        copy = pltpu.make_async_copy(wide.at[d], out_hbm.at[x ^ d], sems.at[d])
        copy.start()
        copies.append(copy)
    for copy in copies:
        copy.wait()


def across(block, bits):
    return lax.ppermute(block, "grp", [(i, i ^ bits) for i in range(lax.axis_size("grp"))])


def limit(mib):
    return pltpu.CompilerParams(vmem_limit_bytes=mib * 2**20)


def in_hbm(array):
    return pltpu.with_memory_space_constraint(array, pltpu.HBM)


def on_device(blocks, own_vectors, over_vectors, neighbours, counts, margin_rows):
    matrix = blocks[0, 0]
    width = matrix.shape[0]
    vectors = own_vectors.shape[2]
    over, rows = over_vectors[0, 0], margin_rows[0, 0]
    message = over.shape[1:]
    f32, bf16 = jnp.float32, jnp.bfloat16

    give, keep = pl.pallas_call(
        pick_kernel,
        out_shape=(pltpu.VMEM((5,) + message, bf16), pltpu.VMEM((3,) + message, bf16)),
        in_specs=[HBM] * 3,
        out_specs=(VMEM, VMEM),
        scratch_shapes=[
            pltpu.SMEM(neighbours.shape[2:], jnp.int32),
            pltpu.SMEM(counts.shape[2:], jnp.int32),
            pltpu.VMEM(over.shape, bf16),
            pltpu.SemaphoreType.DMA((2 + over.shape[0],)),
        ],
        compiler_params=limit(6),
        name="pick",
    )(in_hbm(neighbours[0, 0]), in_hbm(counts[0, 0]), in_hbm(over))
    swap = partner_swap(give)
    size = rows.shape[1] * rows.shape[2]
    hot, mask = pl.pallas_call(
        hot_kernel,
        out_shape=(
            pltpu.VMEM((rows.shape[0], PART, size), bf16),
            pltpu.VMEM((rows.shape[0], width // PART, size), f32),
        ),
        in_specs=[HBM],
        out_specs=(VMEM,) * 2,
        scratch_shapes=[pltpu.VMEM(rows.shape, jnp.int32), pltpu.SemaphoreType.DMA],
        compiler_params=limit(4),
        cost_estimate=pl.CostEstimate(flops=10**9, bytes_accessed=2**24, transcendentals=0),
        name="hot",
    )(in_hbm(rows))
    swap, mask = lax.optimization_barrier((swap, mask))
    two = stream(jnp.stack([keep[2], swap[3], swap[4]]), 2)
    one = stream(jnp.stack([keep[0], swap[1], keep[1], swap[2]]), 1)

    own_present = pl.pallas_call(
        own_kernel,
        out_shape=pltpu.VMEM((2 * vectors, width), bf16),
        in_specs=[HBM, VMEM, VMEM, VMEM],
        out_specs=VMEM,
        scratch_shapes=[pltpu.SemaphoreType.DMA],
        compiler_params=limit(8),
        cost_estimate=pl.CostEstimate(flops=10**9, bytes_accessed=2**24, transcendentals=0),
        name="own",
    )(in_hbm(own_vectors[0, 0]), swap, hot, mask)
    loaded = pltpu.with_memory_space_constraint(matrix, pltpu.VMEM)
    own_product = pl.pallas_call(
        times_kernel,
        out_shape=pltpu.VMEM((2 * vectors, width), bf16),
        in_specs=[VMEM, VMEM],
        out_specs=VMEM,
        compiler_params=limit(8),
        cost_estimate=pl.CostEstimate(flops=10**9, bytes_accessed=2**23, transcendentals=0),
        name="times",
    )(own_present, loaded)
    two, own_product = lax.optimization_barrier((two, own_product))
    pair = pl.pallas_call(
        pair_kernel,
        out_shape=pltpu.VMEM((2 * vectors, width), bf16),
        in_specs=[VMEM] * 3,
        out_specs=VMEM,
        compiler_params=limit(8),
        cost_estimate=pl.CostEstimate(flops=10**9, bytes_accessed=2**23, transcendentals=0),
        name="pair",
    )(hot, mask, two)
    one, pair = lax.optimization_barrier((one, pair))
    post = partner_swap(jnp.concatenate([two[2:3], one[2:4]]))

    near_present, near_product = pl.pallas_call(
        near_kernel,
        out_shape=(pltpu.VMEM((4 * vectors, width), bf16),) * 2,
        in_specs=[VMEM] * 5,
        out_specs=(VMEM,) * 2,
        compiler_params=limit(12),
        cost_estimate=pl.CostEstimate(flops=2 * 10**9, bytes_accessed=2**20, transcendentals=0),
        name="near",
    )(loaded, hot, mask, pair, one)
    post, near_product = lax.optimization_barrier((post, near_product))
    far_present, right, back = pl.pallas_call(
        back_kernel,
        out_shape=(
            pltpu.VMEM((3 * vectors, width), bf16),
            pltpu.VMEM((WIDE * vectors, width), bf16),
            pltpu.VMEM((4, vectors, WIDE * vectors), bf16),
        ),
        in_specs=[VMEM] * 6,
        out_specs=(VMEM,) * 3,
        compiler_params=limit(12),
        cost_estimate=pl.CostEstimate(flops=10**9, bytes_accessed=2**20, transcendentals=0),
        name="back",
    )(own_present, near_present, near_product, hot, mask, post)
    reverse = partner_swap(back)
    home, ahead = pl.pallas_call(
        ahead_kernel,
        out_shape=(
            pltpu.VMEM((2, vectors, WIDE * vectors), f32),
            pltpu.VMEM((3, vectors, WIDE * vectors), f32),
        ),
        in_specs=[VMEM] * 4,
        out_specs=(VMEM,) * 2,
        scratch_shapes=[pltpu.VMEM((5 * vectors, width), bf16)],
        compiler_params=limit(12),
        cost_estimate=pl.CostEstimate(flops=2 * 10**9, bytes_accessed=2**20, transcendentals=0),
        name="ahead",
    )(loaded, own_product, far_present, right)
    reverse, ahead = lax.optimization_barrier((reverse, ahead))
    reverse = reverse.astype(f32)

    far_rows = stream(
        jnp.stack([ahead[2] + reverse[2], reverse[3]]).astype(jnp.bfloat16), 2
    )
    near_rows = stream((ahead[0:2] + reverse[0:2]).astype(jnp.bfloat16), 1)
    row = pltpu.VMEM((vectors, FULL * vectors), f32)
    mine, other = pl.pallas_call(
        window_kernel,
        out_shape=(row, row),
        in_specs=[VMEM, VMEM, VMEM],
        out_specs=(VMEM, VMEM),
        compiler_params=limit(6),
        name="window",
    )(home, near_rows, far_rows)
    coarse = (mine + partner_swap(other)).astype(jnp.bfloat16)

    across_two = across(coarse, 2)
    across_three = across(coarse, 3)
    across_one = across(coarse, 1)
    count = lax.axis_size("grp")
    gathered = pl.pallas_call(
        spread_kernel,
        out_shape=pltpu.HBM((count,) + row.shape, f32),
        in_specs=[VMEM] * 4,
        out_specs=HBM,
        scratch_shapes=[
            pltpu.VMEM((count,) + row.shape, f32),
            pltpu.SemaphoreType.DMA((count,)),
        ],
        compiler_params=limit(6),
        name="spread",
    )(coarse, across_one, across_three, across_two)
    return gathered[:, None]


def solution(mesh):
    placed = (
        P("grp", "sub", None, None),
        P("grp", "sub", None, None),
        P("grp", "sub", None, None, None, None),
        P("grp", "sub", None),
        P("grp", "sub", None),
        P("grp", "sub", None, None, None),
    )
    return jax.shard_map(
        on_device, mesh=mesh, in_specs=placed, out_specs=P(None, "sub", None, None), check_vma=False
    )
```

```python
import jax
import jax.numpy as jnp
from jax import lax
from jax.experimental import pallas as pl
from jax.experimental.pallas import tpu as pltpu
from jax.sharding import PartitionSpec as P

H = 4
SPAN = 2 * H + 1
WIDE = SPAN + 1
FULL = 4 * H + 1
PART = 256
STACK = (0, 1, 2, 3, 4, -1, -2, -3, -4)
VMEM = pl.BlockSpec(memory_space=pltpu.VMEM)
HBM = pl.BlockSpec(memory_space=pltpu.HBM)


def partner_swap(block):
    return lax.ppermute(block, "sub", [(i, i ^ 1) for i in range(lax.axis_size("sub"))])


def stream(block, chips):
    count = lax.axis_size("sub")
    route = []
    for i in range(count):
        target = i + 2 * chips if i % 2 == 0 else i - 2 * chips
        route.append((i, target if 0 <= target < count else i ^ 1))
    return lax.ppermute(block, "sub", route)


def signs():
    me = lax.axis_index("sub")
    core = lax.rem(me, 2)
    return me, core, 1 - 2 * core


def pick_kernel(
    listed_hbm, counts_hbm, over_hbm, swap_ref, keep_ref, listed_ref, counts_ref, over_ref, sems
):
    pairs = [(listed_hbm, listed_ref), (counts_hbm, counts_ref)]
    pairs += [(over_hbm.at[n], over_ref.at[n]) for n in range(over_ref.shape[0])]
    copies = [
        pltpu.make_async_copy(source, target, sems.at[n])
        for n, (source, target) in enumerate(pairs)
    ]
    for copy in copies:
        copy.start()
    for copy in copies:
        copy.wait()
    me, core, sign = signs()
    slots, tiles = over_ref.shape[0], over_ref.shape[1]

    def pick(k, out_ref, at):
        target = me + sign * k
        slot = jnp.int32(0)
        amount = jnp.int32(0)
        for n in range(slots):
            hit = listed_ref[n] == target
            slot = jnp.where(hit, n, slot)
            amount = jnp.where(hit, counts_ref[n], amount)
        for t in range(tiles):
            live = (t < amount).astype(jnp.bfloat16)
            out_ref[at, t] = over_ref[slot, t] * live

    for at, k in enumerate((1, -1, -2, -3, -4)):
        pick(k, swap_ref, at)
    for at, k in enumerate((2, 3, 4)):
        pick(k, keep_ref, at)


def slot_of(sign, k):
    offset = sign * k
    return jnp.where(offset < 0, offset + H, offset + H - 1)


def expand(message, hot, mask):
    tiles, vectors, lanes = message.shape
    flat = jnp.concatenate([message[t] for t in range(tiles)], axis=1)
    parts = mask.shape[0]
    spread = jnp.concatenate(
        [flat * mask[h : h + 1].astype(jnp.bfloat16) for h in range(parts)], axis=0
    )
    dense = lax.dot_general(
        spread, hot, (((1,), (1,)), ((), ())), preferred_element_type=jnp.float32
    ).astype(jnp.bfloat16)
    return [dense[h * vectors : (h + 1) * vectors] for h in range(parts)]


def hot_kernel(rows_hbm, hot_ref, mask_ref, rows_ref, sem):
    copy = pltpu.make_async_copy(rows_hbm, rows_ref, sem)
    copy.start()
    copy.wait()
    lanes = rows_ref.shape[2]
    index = lax.broadcasted_iota(jnp.int32, (PART, lanes), 0)
    parts = lax.broadcasted_iota(jnp.int32, (mask_ref.shape[1], lanes), 0)
    for slot in range(rows_ref.shape[0]):
        low = rows_ref[slot] & (PART - 1)
        high = rows_ref[slot] // PART
        for t in range(rows_ref.shape[1]):
            place = slice(t * lanes, (t + 1) * lanes)
            hot_ref[slot, :, place] = jnp.where(index == low[t : t + 1], 1.0, 0.0).astype(jnp.bfloat16)
            mask_ref[slot, :, place] = jnp.where(parts == high[t : t + 1], 1.0, 0.0)


def own_kernel(own_hbm, swap_ref, hot_ref, mask_ref, present_ref, sem):
    vectors = own_hbm.shape[0]
    own_copy = pltpu.make_async_copy(own_hbm, present_ref.at[pl.ds(0, vectors)], sem)
    own_copy.start()
    me, core, sign = signs()
    slot = slot_of(sign, 1)
    for h, block in enumerate(expand(swap_ref[0], hot_ref[slot], mask_ref[slot])):
        present_ref[vectors:, h * PART : (h + 1) * PART] = block
    own_copy.wait()


def times_kernel(present_ref, matrix_ref, product_ref):
    product_ref[...] = jnp.dot(
        present_ref[...], matrix_ref[...], preferred_element_type=jnp.float32
    ).astype(jnp.bfloat16)


def right_rows(core, k, vectors):
    position = jnp.where(core == 0, H + k, H + 1 - k)
    return pl.ds(pl.multiple_of(position * vectors, vectors), vectors)


def pair_kernel(own_present_ref, hot_ref, mask_ref, two_ref, present_ref, right_ref):
    vectors = two_ref.shape[2]
    me, core, sign = signs()
    right_ref[right_rows(core, H + 1, vectors)] = jnp.zeros(
        (vectors, right_ref.shape[1]), jnp.bfloat16
    )
    for at in range(2):
        right_ref[right_rows(core, at, vectors)] = own_present_ref[at * vectors : (at + 1) * vectors]
    for at, source in enumerate((two_ref.at[1], two_ref.at[0])):
        slot = slot_of(sign, -3 - at)
        for h, block in enumerate(expand(source[...], hot_ref[slot], mask_ref[slot])):
            present_ref[at * vectors : (at + 1) * vectors, h * PART : (h + 1) * PART] = block
            right_ref[right_rows(core, -3 - at, vectors), h * PART : (h + 1) * PART] = block


def near_kernel(matrix_ref, hot_ref, mask_ref, pair_ref, one_ref, present_ref, product_ref):
    vectors = one_ref.shape[2]
    me, core, sign = signs()
    present_ref[2 * vectors :] = pair_ref[...]
    for at, source in enumerate((one_ref.at[1], one_ref.at[0])):
        slot = slot_of(sign, -1 - at)
        for h, block in enumerate(expand(source[...], hot_ref[slot], mask_ref[slot])):
            present_ref[at * vectors : (at + 1) * vectors, h * PART : (h + 1) * PART] = block
    product_ref[...] = jnp.dot(
        present_ref[...], matrix_ref[...], preferred_element_type=jnp.float32
    ).astype(jnp.bfloat16)


def times_all(product, right):
    return lax.dot_general(
        product, right, (((1,), (1,)), ((), ())), preferred_element_type=jnp.float32
    )


def back_kernel(
    early_ref, near_present_ref, near_product_ref, hot_ref, mask_ref, post_ref,
    far_present_ref, right_ref, back_ref,
):
    vectors = post_ref.shape[2]
    width = right_ref.shape[1]
    me, core, sign = signs()

    for at in range(2):
        right_ref[right_rows(core, -1 - at, vectors)] = near_present_ref[at * vectors : (at + 1) * vectors]
    for at, source in enumerate((post_ref.at[2], post_ref.at[1], post_ref.at[0])):
        slot = slot_of(sign, 2 + at)
        for h, block in enumerate(expand(source[...], hot_ref[slot], mask_ref[slot])):
            place = slice(h * PART, (h + 1) * PART)
            far_present_ref[at * vectors : (at + 1) * vectors, place] = block
            right_ref[right_rows(core, 2 + at, vectors), place] = block
    gram = times_all(near_product_ref[...], right_ref[...]).astype(jnp.bfloat16)
    for at in range(4):
        back_ref[at] = gram[at * vectors : (at + 1) * vectors]


def ahead_kernel(
    matrix_ref, own_product_ref, far_present_ref, right_ref, home_ref, ahead_ref, product
):
    vectors = home_ref.shape[1]
    product[0 : 2 * vectors] = own_product_ref[...]
    product[2 * vectors :] = jnp.dot(
        far_present_ref[...], matrix_ref[...], preferred_element_type=jnp.float32
    ).astype(jnp.bfloat16)
    gram = times_all(product[...], right_ref[...])
    for at in range(2):
        home_ref[at] = gram[at * vectors : (at + 1) * vectors]
    for at in range(3):
        ahead_ref[at] = gram[(2 + at) * vectors : (3 + at) * vectors]


def window_kernel(home_ref, one_ref, two_ref, near_ref, far_ref):
    me, core, sign = signs()
    vectors = home_ref.shape[1]
    blocks = FULL

    def window(terms):
        total = None
        for value, start in terms:
            value = value.astype(jnp.float32)
            if start < 0:
                value = value[:, -start * vectors :]
                start = 0
            if start + value.shape[1] // vectors > blocks:
                value = value[:, : (blocks - start) * vectors]
            after = blocks * vectors - start * vectors - value.shape[1]
            value = jnp.pad(value, ((0, 0), (start * vectors, after)))
            total = value if total is None else total + value
        return total

    for c in range(2):
        way = 1 - 2 * c

        @pl.when(core == c)
        def _():
            for ref, at, row in ((near_ref, 0, c), (far_ref, 1, 1 - c)):
                ref[...] = window(
                    [
                        (home_ref[at], H - row),
                        (one_ref[at], H - 2 * way - row),
                        (two_ref[at], H - 4 * way - row),
                    ]
                )


def write_rows(refs, out_hbm, wide, sems):
    x = lax.axis_index("grp")
    copies = []
    for n, (bits, ref) in enumerate(refs):
        wide[n] = ref[...].astype(jnp.float32)
        copy = pltpu.make_async_copy(wide.at[n], out_hbm.at[x ^ bits], sems.at[n])
        copy.start()
        copies.append(copy)
    for copy in copies:
        copy.wait()


def first_kernel(own_ref, two_ref, out_hbm, wide, sems):
    write_rows(((0, own_ref), (2, two_ref)), out_hbm, wide, sems)


def second_kernel(three_ref, one_ref, half_hbm, out_hbm, wide, sems):
    write_rows(((3, three_ref), (1, one_ref)), out_hbm, wide, sems)


def across(block, bits):
    return lax.ppermute(block, "grp", [(i, i ^ bits) for i in range(lax.axis_size("grp"))])


def limit(mib):
    return pltpu.CompilerParams(vmem_limit_bytes=mib * 2**20)


def in_hbm(array):
    return pltpu.with_memory_space_constraint(array, pltpu.HBM)


def on_device(blocks, own_vectors, over_vectors, neighbours, counts, margin_rows):
    matrix = blocks[0, 0]
    width = matrix.shape[0]
    vectors = own_vectors.shape[2]
    over, rows = over_vectors[0, 0], margin_rows[0, 0]
    message = over.shape[1:]
    f32, bf16 = jnp.float32, jnp.bfloat16

    give, keep = pl.pallas_call(
        pick_kernel,
        out_shape=(pltpu.VMEM((5,) + message, bf16), pltpu.VMEM((3,) + message, bf16)),
        in_specs=[HBM] * 3,
        out_specs=(VMEM, VMEM),
        scratch_shapes=[
            pltpu.SMEM(neighbours.shape[2:], jnp.int32),
            pltpu.SMEM(counts.shape[2:], jnp.int32),
            pltpu.VMEM(over.shape, bf16),
            pltpu.SemaphoreType.DMA((2 + over.shape[0],)),
        ],
        compiler_params=limit(6),
        name="pick",
    )(in_hbm(neighbours[0, 0]), in_hbm(counts[0, 0]), in_hbm(over))
    swap = partner_swap(give)
    size = rows.shape[1] * rows.shape[2]
    hot, mask = pl.pallas_call(
        hot_kernel,
        out_shape=(
            pltpu.VMEM((rows.shape[0], PART, size), bf16),
            pltpu.VMEM((rows.shape[0], width // PART, size), f32),
        ),
        in_specs=[HBM],
        out_specs=(VMEM,) * 2,
        scratch_shapes=[pltpu.VMEM(rows.shape, jnp.int32), pltpu.SemaphoreType.DMA],
        compiler_params=limit(4),
        cost_estimate=pl.CostEstimate(flops=10**9, bytes_accessed=2**24, transcendentals=0),
        name="hot",
    )(in_hbm(rows))
    swap, mask = lax.optimization_barrier((swap, mask))
    two = stream(jnp.stack([keep[2], swap[3], swap[4]]), 2)
    one = stream(jnp.stack([keep[0], swap[1], keep[1], swap[2]]), 1)

    own_present = pl.pallas_call(
        own_kernel,
        out_shape=pltpu.VMEM((2 * vectors, width), bf16),
        in_specs=[HBM, VMEM, VMEM, VMEM],
        out_specs=VMEM,
        scratch_shapes=[pltpu.SemaphoreType.DMA],
        compiler_params=limit(8),
        cost_estimate=pl.CostEstimate(flops=10**9, bytes_accessed=2**24, transcendentals=0),
        name="own",
    )(in_hbm(own_vectors[0, 0]), swap, hot, mask)
    loaded = pltpu.with_memory_space_constraint(matrix, pltpu.VMEM)
    own_product = pl.pallas_call(
        times_kernel,
        out_shape=pltpu.VMEM((2 * vectors, width), bf16),
        in_specs=[VMEM, VMEM],
        out_specs=VMEM,
        compiler_params=limit(8),
        cost_estimate=pl.CostEstimate(flops=10**9, bytes_accessed=2**23, transcendentals=0),
        name="times",
    )(own_present, loaded)
    two, own_product = lax.optimization_barrier((two, own_product))
    pair, early = pl.pallas_call(
        pair_kernel,
        out_shape=(
            pltpu.VMEM((2 * vectors, width), bf16),
            pltpu.VMEM((WIDE * vectors, width), bf16),
        ),
        in_specs=[VMEM] * 4,
        out_specs=(VMEM,) * 2,
        compiler_params=limit(8),
        cost_estimate=pl.CostEstimate(flops=10**9, bytes_accessed=2**23, transcendentals=0),
        name="pair",
    )(own_present, hot, mask, two)
    one, pair = lax.optimization_barrier((one, pair))
    post = partner_swap(jnp.concatenate([two[2:3], one[2:4]]))

    near_present, near_product = pl.pallas_call(
        near_kernel,
        out_shape=(pltpu.VMEM((4 * vectors, width), bf16),) * 2,
        in_specs=[VMEM] * 5,
        out_specs=(VMEM,) * 2,
        compiler_params=limit(12),
        cost_estimate=pl.CostEstimate(flops=2 * 10**9, bytes_accessed=2**20, transcendentals=0),
        name="near",
    )(loaded, hot, mask, pair, one)
    post, near_product = lax.optimization_barrier((post, near_product))
    far_present, right, back = pl.pallas_call(
        back_kernel,
        out_shape=(
            pltpu.VMEM((3 * vectors, width), bf16),
            pltpu.VMEM((WIDE * vectors, width), bf16),
            pltpu.VMEM((4, vectors, WIDE * vectors), bf16),
        ),
        in_specs=[VMEM] * 6,
        out_specs=(VMEM,) * 3,
        compiler_params=limit(12),
        cost_estimate=pl.CostEstimate(flops=10**9, bytes_accessed=2**20, transcendentals=0),
        input_output_aliases={0: 1},
        name="back",
    )(early, near_present, near_product, hot, mask, post)
    reverse = partner_swap(back)
    home, ahead = pl.pallas_call(
        ahead_kernel,
        out_shape=(
            pltpu.VMEM((2, vectors, WIDE * vectors), f32),
            pltpu.VMEM((3, vectors, WIDE * vectors), f32),
        ),
        in_specs=[VMEM] * 4,
        out_specs=(VMEM,) * 2,
        scratch_shapes=[pltpu.VMEM((5 * vectors, width), bf16)],
        compiler_params=limit(12),
        cost_estimate=pl.CostEstimate(flops=2 * 10**9, bytes_accessed=2**20, transcendentals=0),
        name="ahead",
    )(loaded, own_product, far_present, right)
    reverse, ahead = lax.optimization_barrier((reverse, ahead))
    reverse = reverse.astype(f32)

    far_rows = stream(
        jnp.stack([ahead[2] + reverse[2], reverse[3]]).astype(jnp.bfloat16), 2
    )
    near_rows = stream((ahead[0:2] + reverse[0:2]).astype(jnp.bfloat16), 1)
    row = pltpu.VMEM((vectors, FULL * vectors), f32)
    mine, other = pl.pallas_call(
        window_kernel,
        out_shape=(row, row),
        in_specs=[VMEM, VMEM, VMEM],
        out_specs=(VMEM, VMEM),
        compiler_params=limit(6),
        name="window",
    )(home, near_rows, far_rows)
    coarse = (mine + partner_swap(other)).astype(jnp.bfloat16)

    across_two = across(coarse, 2)
    across_three = across(coarse, 3)
    across_one = across(coarse, 1)
    count = lax.axis_size("grp")
    scratch = [pltpu.VMEM((2,) + row.shape, f32), pltpu.SemaphoreType.DMA((2,))]
    half = pl.pallas_call(
        first_kernel,
        out_shape=pltpu.HBM((count,) + row.shape, f32),
        in_specs=[VMEM] * 2,
        out_specs=HBM,
        scratch_shapes=scratch,
        compiler_params=limit(6),
        cost_estimate=pl.CostEstimate(flops=10**6, bytes_accessed=2**20, transcendentals=0),
        name="first",
    )(coarse, across_two)
    across_three, half = lax.optimization_barrier((across_three, half))
    gathered = pl.pallas_call(
        second_kernel,
        out_shape=pltpu.HBM((count,) + row.shape, f32),
        in_specs=[VMEM, VMEM, HBM],
        out_specs=HBM,
        scratch_shapes=scratch,
        input_output_aliases={2: 0},
        compiler_params=limit(6),
        name="second",
    )(across_three, across_one, in_hbm(half))
    return gathered[:, None]


def solution(mesh):
    placed = (
        P("grp", "sub", None, None),
        P("grp", "sub", None, None),
        P("grp", "sub", None, None, None, None),
        P("grp", "sub", None),
        P("grp", "sub", None),
        P("grp", "sub", None, None, None),
    )
    return jax.shard_map(
        on_device, mesh=mesh, in_specs=placed, out_specs=P(None, "sub", None, None), check_vma=False
    )
```
